512 devices in a mesh: seq: 32 (over x, y), head: 16 (over z, core).
Axes of the slice: x: 4, y: 8, z: 8, core: 2. Of those that a mesh axis runs over, the one named last changes fastest.
Arguments:
- ssm_input: bfloat16 [6144, 16384], P('seq', 'head'), may hold values from -6 to 6
- state_in: bfloat16 [6144, 2048], P('seq'), may hold values from -0.375 to 0.375
- state_out: bfloat16 [6144, 2048], P('seq'), may hold values from -0.078125 to 0.078125
- step_size: float32 [6144, 256], P('seq', 'head'), may hold values from 0.5 to 1.5
- decay_rate: float32 [256], P('head'), may hold values from 8.138021e-06 to 0.04
- forget: float32 [6144], P('seq'), may hold values from 0 to 0.9
- skip_gain: float32 [256], P('head'), may hold values from 0.25 to 1.75
- queries: bfloat16 [6144, 8192], P('seq', 'head'), may hold values from -48 to 48
- new_keys: bfloat16 [6144, 1024], P('seq'), may hold values from -6 to 6
- new_values: bfloat16 [6144, 1024], P('seq'), may hold values from -6 to 6
- cache_keys: bfloat16 [4096, 1024], P('seq'), may hold values from -127 to 127, as said below
- cache_values: bfloat16 [4096, 1024], P('seq'), may hold values from -127 to 127, as said below
- cache_key_scale: float32 [1024], replicated, may hold values from 0.003 to 0.03
- cache_value_scale: float32 [1024], replicated, may hold values from 0.003 to 0.03
Outputs:
- ssm_output: bfloat16 [6144, 16384], P('seq', 'head')
- attended: bfloat16 [6144, 8192], P('seq', 'head')
- key_codes: bfloat16 [6144, 1024], P('seq')
- key_scale: float32 [1024], replicated
The draws below stay inside these ranges and needn't reach their ends.
Inputs may be any that keep to these rules, and one draw needn't show every extreme that they name: `cache_keys`: whole numbers. `cache_values`: whole numbers.
All inputs are finite; a program needn't handle non-finite values.
Results may differ from the reference program's by a relative error of at most 0.019.
Values may be sent and summed in bfloat16 or wider, within the bound.
No kernel may reach another device: no remote copies, remote signals or barrier semaphores. Data moves between devices by JAX's collectives and lax.ppermute only.
A program may use at most 128 MiB of HBM per device.

```python
import math
import jax
import jax.numpy as jnp
from jax import lax

SSM_HEADS = 256
HEAD_DIM = 64
STATE = 256
GROUPS = 8
ATT_HEADS = 64
KV_HEADS = 8
ATT_DIM = 128
TOK_DEV = 192
TOKENS = 6144
CACHE = 4096


def draw_decay_rate(key, part):
    key_a, key_b, key_c = jax.random.split(jax.random.fold_in(key, 11), 3)
    slow = jnp.exp(jax.random.uniform(key_a, (SSM_HEADS,), minval=math.log(0.05 / TOKENS), maxval=math.log(0.4 / TOKENS)))
    quick = jax.random.uniform(key_b, (SSM_HEADS,), minval=0.02, maxval=0.04)
    share = 0.5
    picked = jax.random.uniform(key_c, (SSM_HEADS,)) < share
    return jnp.where(picked, quick, slow).astype(jnp.float32)


def draw_forget(key, part):
    key_a, key_b = jax.random.split(jax.random.fold_in(key, 12), 2)
    spots = jax.random.randint(key_a, (4,), 0, TOKENS)
    amount = jax.random.uniform(key_b, (4,), minval=0.2, maxval=0.4)
    hits = (jnp.arange(TOKENS, dtype=jnp.int32)[:, None] == spots[None, :]).astype(jnp.float32)
    return jnp.dot(hits, amount).astype(jnp.float32)


def draw_queries(key, part):
    key_a = jax.random.fold_in(jax.random.fold_in(key, 13), 0)
    base = jax.random.normal(key_a, (TOKENS, ATT_HEADS * ATT_DIM))
    return jnp.clip(base, -48.0, 48.0).astype(jnp.bfloat16)


def cache_codes(key):
    spread = jax.random.uniform(key, (CACHE, KV_HEADS * ATT_DIM), minval=-127.0, maxval=127.0)
    return jnp.clip(jnp.floor(spread + 0.5), -127.0, 127.0).astype(jnp.bfloat16)


def draw_cache_keys(key, part):
    return cache_codes(jax.random.fold_in(key, 14))


def draw_cache_values(key, part):
    return cache_codes(jax.random.fold_in(key, 15))


def block_scale(own_key, dims, cuts, smallest, high):
    factor_of, own = 1.0, jax.random.fold_in(own_key, 6)
    for axis_at, parts in cuts:
        draws = jnp.exp(jax.random.uniform(jax.random.fold_in(own, axis_at), (parts,), jnp.float32, smallest / len(cuts), high / len(cuts)))
        factor_of = factor_of * jnp.repeat(draws, dims[axis_at] // parts).reshape([-1 if axis == axis_at else 1 for axis in range(len(dims))])
    return factor_of


def bell_draw(key, shape, scale, limit, pieces=(), kind=jnp.bfloat16):
    array = scale * jax.random.normal(key, shape, jnp.float32)
    if pieces:
        array = array * block_scale(key, shape, pieces, -0.22, 0.18)
    return jnp.clip(array, -limit, limit).astype(kind)


def setup_inputs(seed: int = 0) -> dict:
    key_list = jax.random.split(jax.random.key(seed), 15)
    return {
        "ssm_input": bell_draw(key_list[0], (TOKENS, SSM_HEADS * HEAD_DIM), 1.0, 6.0, ((0, 32), (1, 16))),
        "state_in": bell_draw(key_list[1], (TOKENS, GROUPS * STATE), STATE ** -0.5, 0.375, ((0, 32),)),
        "state_out": bell_draw(key_list[2], (TOKENS, GROUPS * STATE), TOKENS ** -0.5, 0.078125, ((0, 32),)),
        "step_size": jnp.clip(0.5 + 1.0 * jax.random.uniform(key_list[3], (TOKENS, SSM_HEADS), jnp.float32) ** block_scale(key_list[3], (TOKENS, SSM_HEADS), ((0, 32), (1, 16)), -0.2, 0.2), 0.5, 1.5),
        "decay_rate": draw_decay_rate(jax.random.fold_in(key_list[14], 71), 0),
        "forget": draw_forget(jax.random.fold_in(key_list[14], 71), 0),
        "skip_gain": jnp.clip(1.0 + 0.15 * jax.random.normal(key_list[6], (SSM_HEADS,), jnp.float32), 0.25, 1.75),
        "queries": draw_queries(jax.random.fold_in(key_list[14], 71), 0),
        "new_keys": bell_draw(key_list[8], (TOKENS, KV_HEADS * ATT_DIM), 1.0, 6.0, ((0, 32),)),
        "new_values": bell_draw(key_list[9], (TOKENS, KV_HEADS * ATT_DIM), 1.0, 6.0, ((0, 32),)),
        "cache_keys": draw_cache_keys(jax.random.fold_in(key_list[14], 71), 0),
        "cache_values": draw_cache_values(jax.random.fold_in(key_list[14], 71), 0),
        "cache_key_scale": jnp.clip(jnp.exp(jax.random.uniform(key_list[12], (KV_HEADS * ATT_DIM,), jnp.float32, math.log(0.003), math.log(0.03))), 0.003, 0.03),
        "cache_value_scale": jnp.clip(jnp.exp(jax.random.uniform(key_list[13], (KV_HEADS * ATT_DIM,), jnp.float32, math.log(0.003), math.log(0.03))), 0.003, 0.03),
    }


NEG = -1.0e30


def head_maps(maps, choose):
    highest = lax.Precision.HIGHEST
    length = maps.shape[0]
    grouped = maps.reshape(length, GROUPS, STATE)
    return jnp.einsum('tgn,hg->thn', grouped, choose, precision=highest)


def span_parts(rate, inputs, in_heads, out_heads):
    highest = lax.Precision.HIGHEST
    length = rate.shape[0]
    lower = jnp.tril(jnp.ones((length, length), jnp.float32))
    running = jnp.dot(lower, rate, precision=highest)
    gram = jnp.einsum('thn,shn->hts', out_heads, in_heads, precision=highest)
    across = running.T
    spread = across[:, :, None] - across[:, None, :]
    causal = lower[None, :, :] > 0.0
    weight = jnp.where(causal, jnp.exp(jnp.where(causal, spread, 0.0)), 0.0) * gram
    within = jnp.einsum('hts,shp->thp', weight, inputs, precision=highest)
    final = running[length - 1]
    tail = jnp.exp(final[None, :] - running)
    local = jnp.einsum('sh,shp,shn->hpn', tail, inputs, in_heads, precision=highest)
    return running, within, local, jnp.exp(final)


def prior_term(running, out_heads, carried):
    highest = lax.Precision.HIGHEST
    return jnp.exp(running)[:, :, None] * jnp.einsum('thn,hpn->thp', out_heads, carried, precision=highest)


def ssd_layer(ssm_input, state_in, state_out, step_size, decay_rate, forget, skip_gain):
    blocks = TOKENS // TOK_DEV
    rate = -decay_rate[None, :] * step_size - forget[:, None]
    signal = ssm_input.astype(jnp.float32).reshape(TOKENS, SSM_HEADS, HEAD_DIM)
    inputs = signal * step_size[:, :, None]
    head_group = jnp.arange(SSM_HEADS, dtype=jnp.int32) // (SSM_HEADS // GROUPS)
    choose = (head_group[:, None] == jnp.arange(GROUPS, dtype=jnp.int32)[None, :]).astype(jnp.float32)

    def advance(carried, item):
        rate_b, input_b, in_b, out_b, signal_b = item
        in_heads = head_maps(in_b, choose)
        out_heads = head_maps(out_b, choose)
        running, within, local, decay = span_parts(rate_b, input_b, in_heads, out_heads)
        mixed = within + prior_term(running, out_heads, carried) + skip_gain[None, :, None] * signal_b
        carried = decay[:, None, None] * carried + local
        return carried, mixed

    start = jnp.zeros((SSM_HEADS, HEAD_DIM, STATE), jnp.float32)
    items = (rate.reshape(blocks, TOK_DEV, SSM_HEADS),
             inputs.reshape(blocks, TOK_DEV, SSM_HEADS, HEAD_DIM),
             state_in.astype(jnp.float32).reshape(blocks, TOK_DEV, GROUPS * STATE),
             state_out.astype(jnp.float32).reshape(blocks, TOK_DEV, GROUPS * STATE),
             signal.reshape(blocks, TOK_DEV, SSM_HEADS, HEAD_DIM))
    _, mixed = lax.scan(advance, start, items)
    return mixed.reshape(TOKENS, SSM_HEADS * HEAD_DIM).astype(jnp.bfloat16)


def attention_layer(queries, new_keys, new_values, cache_keys, cache_values, cache_key_scale, cache_value_scale):
    cache_k = (cache_keys.astype(jnp.float32) * cache_key_scale[None, :]).astype(jnp.bfloat16)
    cache_v = (cache_values.astype(jnp.float32) * cache_value_scale[None, :]).astype(jnp.bfloat16)
    keys = jnp.concatenate([cache_k, new_keys], axis=0).reshape(CACHE + TOKENS, KV_HEADS, ATT_DIM)
    values = jnp.concatenate([cache_v, new_values], axis=0).reshape(CACHE + TOKENS, KV_HEADS, ATT_DIM)
    heads = queries.reshape(TOKENS, ATT_HEADS, ATT_DIM)
    group = ATT_HEADS // KV_HEADS
    key_pos = jnp.arange(CACHE + TOKENS, dtype=jnp.int32)
    query_pos = CACHE + jnp.arange(TOKENS, dtype=jnp.int32)
    visible = key_pos[None, :] <= query_pos[:, None]

    def one_head(index):
        query = lax.dynamic_index_in_dim(heads, index, axis=1, keepdims=False)
        key_head = lax.dynamic_index_in_dim(keys, index // group, axis=1, keepdims=False)
        value_head = lax.dynamic_index_in_dim(values, index // group, axis=1, keepdims=False)
        scores = jnp.dot(query, key_head.T, preferred_element_type=jnp.float32) * (ATT_DIM ** -0.5)
        scores = jnp.where(visible, scores, NEG)
        peak = jnp.max(scores, axis=1, keepdims=True)
        weights = jnp.where(visible, jnp.exp(scores - peak), 0.0)
        total = jnp.sum(weights, axis=1, keepdims=True)
        summed = jnp.dot(weights.astype(jnp.bfloat16), value_head, preferred_element_type=jnp.float32)
        return (summed / total).astype(jnp.bfloat16)

    outputs = lax.map(one_head, jnp.arange(ATT_HEADS, dtype=jnp.int32))
    return outputs.transpose(1, 0, 2).reshape(TOKENS, ATT_HEADS * ATT_DIM)


def reference(ssm_input, state_in, state_out, step_size, decay_rate, forget, skip_gain, queries, new_keys, new_values, cache_keys, cache_values, cache_key_scale, cache_value_scale):
    ssm_output = ssd_layer(ssm_input, state_in, state_out, step_size, decay_rate, forget, skip_gain)
    attended = attention_layer(queries, new_keys, new_values, cache_keys, cache_values, cache_key_scale, cache_value_scale)
    magnitude = jnp.max(jnp.abs(new_keys.astype(jnp.float32)), axis=0)
    key_scale = (magnitude + 1e-6) / 127.0
    key_codes = (new_keys.astype(jnp.float32) / key_scale[None, :]).astype(jnp.bfloat16)
    return ssm_output, attended, key_codes, key_scale
```

```python
import functools

import jax
import jax.numpy as jnp
from jax import lax
from jax.experimental import pallas as pl
from jax.experimental.pallas import tpu as pltpu
from jax.sharding import Mesh
from jax.sharding import PartitionSpec as P

SSM_HEADS = 256
HEAD_DIM = 64
STATE = 256
GROUPS = 8
ATT_HEADS = 64
KV_HEADS = 8
ATT_DIM = 128
SEQ = ("seq_0", "seq_1")
NX, NY, ND = 4, 8, 32

TOK = 192
CROWS = 64
NROWS = 96
HALF = CROWS + NROWS
HEADS = 16
COLS = HEADS * HEAD_DIM
QH = 4
ROWS = QH * TOK
STAT = 32
SLOT = 80
NEG = -1e30
LOG2E = 1.4426950408889634
SCALE = ATT_DIM**-0.5 * LOG2E
F32 = jnp.float32
BF16 = jnp.bfloat16
HIGHEST = lax.Precision.HIGHEST


def whole():
    return pl.BlockSpec(memory_space=pltpu.VMEM)


def call(kernel, out_shape, args, name, flops, scratch=(), moved=1 << 21):
    return pl.pallas_call(
        kernel,
        out_shape=out_shape,
        in_specs=[pl.BlockSpec(memory_space=pltpu.SMEM)] + [whole()] * (len(args) - 1),
        out_specs=jax.tree.map(lambda _: whole(), out_shape),
        scratch_shapes=list(scratch),
        compiler_params=pltpu.CompilerParams(vmem_limit_bytes=56 << 20),
        cost_estimate=pl.CostEstimate(flops=flops, bytes_accessed=moved, transcendentals=0),
        name=name,
    )(*args)


def parts_of(value):
    hi = value.astype(BF16)
    left = value - hi.astype(F32)
    mid = left.astype(BF16)
    low = (left - mid.astype(F32)).astype(BF16)
    return hi, mid, low


def spread_heads(per_head):
    rows = per_head.shape[0]
    low = lax.broadcasted_iota(jnp.int32, (rows, 128), 1) < HEAD_DIM
    tiles = []
    for j in range(HEADS // 2):
        tiles.append(
            jnp.where(low, per_head[:, 2 * j : 2 * j + 1], per_head[:, 2 * j + 1 : 2 * j + 2])
        )
    return jnp.concatenate(tiles, axis=1)


def pack_kernel(place, ck, cv, nk, nv, ks, vs, out):
    keys = (ck[...].astype(F32) * ks[...]).astype(BF16)
    values = (cv[...].astype(F32) * vs[...]).astype(BF16)
    cache = jnp.concatenate([keys, values], axis=1)
    fresh = jnp.concatenate([nk[...], nv[...]], axis=1)
    for k in range(NY):
        out[k, :CROWS, :] = cache
        out[k, CROWS:, :] = fresh


def pack(place, ck, cv, nk, nv, ks, vs):
    row = lambda i, p: (p[3], p[2])
    top = lambda i, p: (0, p[2])
    return pl.pallas_call(
        pack_kernel,
        out_shape=jax.ShapeDtypeStruct((NY, HALF, 2 * ATT_DIM), BF16),
        grid_spec=pltpu.PrefetchScalarGridSpec(
            num_scalar_prefetch=1,
            grid=(1,),
            in_specs=[
                pl.BlockSpec((CROWS, ATT_DIM), row),
                pl.BlockSpec((CROWS, ATT_DIM), row),
                pl.BlockSpec((NROWS, ATT_DIM), row),
                pl.BlockSpec((NROWS, ATT_DIM), row),
                pl.BlockSpec((1, ATT_DIM), top),
                pl.BlockSpec((1, ATT_DIM), top),
            ],
            out_specs=pl.BlockSpec((NY, HALF, 2 * ATT_DIM), lambda i, p: (0, 0, 0)),
        ),
        cost_estimate=pl.CostEstimate(flops=1000000, bytes_accessed=1 << 20, transcendentals=0),
        name="pack",
    )(place, ck, cv, nk, nv, ks, vs)


def local_kernel(place, x, step, b_map, rate_of, forget, nk, send, run_out, run_t_out):
    rows = lax.broadcasted_iota(jnp.int32, (TOK, TOK), 0)
    cols = lax.broadcasted_iota(jnp.int32, (TOK, TOK), 1)
    lost = jnp.sum(jnp.where(rows == cols, forget[...], 0.0), axis=1, keepdims=True)
    rate = -rate_of[...] * step[...] - lost
    lower = (rows >= cols).astype(F32)
    running = jnp.dot(lower, rate, precision=HIGHEST, preferred_element_type=F32)
    run_out[...] = running
    run_t_out[...] = lax.dot_general(
        rate,
        (rows <= cols).astype(F32),
        (((0,), (0,)), ((), ())),
        precision=HIGHEST,
        preferred_element_type=F32,
    )
    final = running[TOK - 1 : TOK, :]
    gain = spread_heads(jnp.exp(final - running) * step[...])
    given = (x[...].astype(F32) * gain).astype(BF16)
    local = lax.dot_general(
        b_map[...], given, (((0,), (0,)), ((), ())), preferred_element_type=F32
    ).astype(BF16)
    decay = spread_heads(jnp.exp(jnp.broadcast_to(final, (8, HEADS))))[0:1, :]
    hi = decay.astype(BF16)
    low = (decay - hi.astype(F32)).astype(BF16)
    peak = jnp.max(jnp.abs(nk[...].astype(F32)), axis=0, keepdims=True)
    blank = jnp.zeros((7, ATT_DIM), F32)
    for d in range(ND):
        block, half = d // 2, d % 2
        tail = []
        for source in (hi, low):
            for j in range(4):
                at = (half * 4 + j) * 128
                tail.append(source[:, at : at + 128].astype(F32))
        tile = d // 4
        tail.append(peak[:, tile * 128 : tile * 128 + 128])
        tail.append(blank)
        for j in range(4):
            at = (half * 4 + j) * 128
            send[d, 16 * j : 16 * j + 16, :] = local[16 * block : 16 * block + 16, at : at + 128]
        send[d, 64:80, :] = jnp.concatenate(tail, axis=0).astype(BF16)


def within_kernel(place, x, step, running, run_t, b_map, c_map, skip, base):
    rows = lax.broadcasted_iota(jnp.int32, (TOK, TOK), 0)
    cols = lax.broadcasted_iota(jnp.int32, (TOK, TOK), 1)
    causal = rows >= cols
    gram = lax.dot_general(
        c_map[...], b_map[...], (((1,), (1,)), ((), ())), preferred_element_type=F32
    )
    signal = x[...].astype(F32)
    given = (signal * spread_heads(step[...])).astype(BF16)
    skips = spread_heads(jnp.broadcast_to(skip[...], (8, HEADS)))[0:1, :]
    low = lax.broadcasted_iota(jnp.int32, (TOK, 128), 1) < HEAD_DIM
    for j in range(HEADS // 2):
        sides = []
        part = given[:, 128 * j : 128 * j + 128]
        for h in (2 * j, 2 * j + 1):
            spread = running[:, h : h + 1] - run_t[h : h + 1, :]
            weight = jnp.exp(jnp.where(causal, spread, NEG)) * gram
            sides.append(jnp.dot(weight.astype(BF16), part, preferred_element_type=F32))
        at = slice(128 * j, 128 * j + 128)
        base[:, at] = jnp.where(low, sides[0], sides[1]) + skips[:, at] * signal[:, at]


def scan_kernel(place, recv, send):
    states = [jnp.zeros((16, 128), F32) for _ in range(4)]
    peak = jnp.max(recv[:, 64:80, :].astype(F32), axis=0)[8:9, :]
    peak = jnp.broadcast_to(peak, (16, 128)).astype(BF16)
    for s in range(ND):
        tail = recv[s, 64:80, :].astype(F32)
        for j in range(4):
            send[s, 16 * j : 16 * j + 16, :] = states[j].astype(BF16)
            decay = tail[j : j + 1, :] + tail[4 + j : 5 + j, :]
            states[j] = decay * states[j] + recv[s, 16 * j : 16 * j + 16, :].astype(F32)
        send[s, 64:80, :] = peak


def final_kernel(place, recv, base, c_map, running, nk, out, codes, scale, carried):
    for d in range(ND):
        block, half = d // 2, d % 2
        for j in range(4):
            at = (half * 4 + j) * 128
            carried[16 * block : 16 * block + 16, at : at + 128] = recv[d, 16 * j : 16 * j + 16, :]
    prior = jnp.dot(c_map[...], carried[...], preferred_element_type=F32)
    out[...] = (base[...] + spread_heads(jnp.exp(running[...])) * prior).astype(BF16)
    peak = jnp.concatenate([recv[4 * t, 64:80, :].astype(F32)[0:1, :] for t in range(8)], axis=1)
    key_scale = (peak + 1e-6) / 127.0
    scale[...] = key_scale
    codes[...] = (nk[...].astype(F32) / key_scale).astype(BF16)


def load_keys(kv_a, kv_b, keys, values):
    at = 0
    for first, count in ((0, CROWS), (CROWS, NROWS)):
        for ref in (kv_a, kv_b):
            size = NY * count
            both = ref[:, first : first + count, :].reshape(size, 2 * ATT_DIM)
            keys[at : at + size, :] = both[:, :ATT_DIM]
            values[at : at + size, :ATT_DIM] = both[:, ATT_DIM:]
            at += size
    values[:, ATT_DIM:] = jnp.ones((NY * 2 * HALF, ATT_DIM), BF16)


CACHED = 2 * NY * CROWS
FRESH = 2 * NY * NROWS


def scores_of(q, keys):
    return lax.dot_general(q, keys, (((1,), (1,)), ((), ())), preferred_element_type=F32)


def attend_kernel(offsets, place, *refs):
    count = len(offsets)
    queries, kv_a, kv_b = refs[:count], refs[count], refs[count + 1]
    outs = refs[count + 2 : 2 * count + 2]
    keys, values, q_rows, sums = refs[2 * count + 2 :]
    mine = place[0]
    load_keys(kv_a, kv_b, keys, values)
    for b in range(count):
        for h in range(QH):
            q_rows[(b * QH + h) * TOK : (b * QH + h + 1) * TOK, :] = queries[b][
                :, h * ATT_DIM : (h + 1) * ATT_DIM
            ]

    def finish(at, summed, top):
        total = summed[:, ATT_DIM:]
        sums[pl.ds(at, TOK), :ATT_DIM] = summed[:, :ATT_DIM] / total
        sums[pl.ds(at, TOK), ATT_DIM:] = top * SCALE + jnp.log2(total)

    def tile(at, owner):
        q = q_rows[pl.ds(at, TOK), :]
        old = scores_of(q, keys[:CACHED, :])
        old_top = jnp.max(old, axis=1, keepdims=True)

        @pl.when(owner < mine)
        def _():
            probs = jnp.exp2(old * SCALE - old_top * SCALE).astype(BF16)
            summed = jnp.dot(probs, values[:CACHED, :], preferred_element_type=F32)
            finish(at, summed, old_top)

        @pl.when(owner >= mine)
        def _():
            new = scores_of(q, keys[CACHED:, :])
            if offsets == (0,):
                col = lax.broadcasted_iota(jnp.int32, (1, FRESH), 1)
                blocks = jnp.zeros((1, FRESH), jnp.int32)
                for k in range(1, 2 * NY):
                    blocks += (col >= k * NROWS).astype(jnp.int32)
                second = (col >= FRESH // 2).astype(jnp.int32)
                side = jnp.where(second == 1, 1 - place[3], place[3])
                pos = col + (blocks + side) * NROWS - second * (2 * NY * NROWS)
                row = lax.broadcasted_iota(jnp.int32, (TOK, 1), 0) + place[1] * TOK
                seen = pos <= row
                new = jnp.where(seen, new, NEG)
            top = jnp.maximum(old_top, jnp.max(new, axis=1, keepdims=True))
            fixed = top * SCALE
            probs = jnp.exp2(old * SCALE - fixed).astype(BF16)
            summed = jnp.dot(probs, values[:CACHED, :], preferred_element_type=F32)
            weights = jnp.exp2(new * SCALE - fixed)
            if offsets == (0,):
                weights = jnp.where(seen, weights, 0.0)
            summed += jnp.dot(
                weights.astype(BF16), values[CACHED:, :], preferred_element_type=F32
            )
            finish(at, summed, top)

    for b in range(count):
        owner = lax.rem(mine + offsets[b] + NX, NX)

        @pl.loop(0, QH)
        def _(h):
            tile(pl.multiple_of((b * QH + h) * TOK, TOK), owner)

    diagonal = lax.broadcasted_iota(jnp.int32, (128, 128), 0) == lax.broadcasted_iota(
        jnp.int32, (128, 128), 1
    )
    for b in range(count):
        outs[b][:ROWS, :] = sums[b * ROWS : (b + 1) * ROWS, :ATT_DIM].astype(BF16)
        lines = []
        for k in range(ROWS // 128):
            block = sums[b * ROWS + k * 128 : b * ROWS + k * 128 + 128, ATT_DIM:]
            lines.append(jnp.sum(jnp.where(diagonal, block, 0.0), axis=0, keepdims=True))
        lines.append(jnp.zeros((2, ATT_DIM), F32))
        stats = jnp.concatenate(lines, axis=0)
        hi, mid, low = parts_of(stats)
        packed = jnp.concatenate(
            [hi.astype(F32), mid.astype(F32), low.astype(F32), jnp.zeros((8, ATT_DIM), F32)], axis=0
        )
        outs[b][ROWS:, :] = packed.astype(BF16)


def attend(place, queries, kv_a, kv_b, offsets, name):
    count = len(offsets)
    partial = jax.ShapeDtypeStruct((ROWS + STAT, ATT_DIM), BF16)
    return call(
        functools.partial(attend_kernel, offsets),
        [partial] * count,
        (place, *queries, kv_a, kv_b),
        name,
        count * 4 * ROWS * (CACHED + FRESH) * ATT_DIM,
        scratch=(
            pltpu.VMEM((CACHED + FRESH, ATT_DIM), BF16),
            pltpu.VMEM((CACHED + FRESH, 2 * ATT_DIM), BF16),
            pltpu.VMEM((count * ROWS, ATT_DIM), BF16),
            pltpu.VMEM((count * ROWS, 2 * ATT_DIM), F32),
        ),
    )


def merge_kernel(place, *refs):
    parts, out = refs[:-1], refs[-1]
    diagonal = lax.broadcasted_iota(jnp.int32, (128, 128), 0) == lax.broadcasted_iota(
        jnp.int32, (128, 128), 1
    )
    stats = []
    for ref in parts:
        packed = ref[ROWS:, :].astype(F32)
        stats.append(packed[0:8] + packed[8:16] + packed[16:24])
    top = functools.reduce(jnp.maximum, stats)
    shares = [jnp.exp2(s - top) for s in stats]
    total = functools.reduce(jnp.add, shares)
    shares = [s / total for s in shares]
    pieces = []
    for k in range(ROWS // 128):
        summed = jnp.zeros((128, 128), F32)
        for share, ref in zip(shares, parts):
            line = jnp.where(diagonal, share[k : k + 1, :], 0.0)
            column = jnp.sum(line, axis=1, keepdims=True)
            summed += column * ref[k * 128 : k * 128 + 128, :].astype(F32)
        pieces.append(summed)
    result = jnp.concatenate(pieces, axis=0)
    for h in range(QH):
        out[:, h * ATT_DIM : (h + 1) * ATT_DIM] = result[h * TOK : (h + 1) * TOK, :].astype(BF16)


def shift(value, axis, by):
    size = lax.axis_size(axis)
    return lax.ppermute(value, axis, [(i, (i + by) % size) for i in range(size)])


def body(
    ssm_input,
    state_in,
    state_out,
    step_size,
    decay_rate,
    forget,
    skip_gain,
    queries,
    new_keys,
    new_values,
    cache_keys,
    cache_values,
    cache_key_scale,
    cache_value_scale,
):
    head = lax.axis_index("head")
    column, core = head // 2, head % 2
    place = jnp.stack(
        [lax.axis_index("seq_0"), lax.axis_index("seq_1"), column, core]
    ).astype(jnp.int32)

    packed = pack(
        place,
        cache_keys,
        cache_values,
        new_keys,
        new_values,
        cache_key_scale.reshape(1, -1),
        cache_value_scale.reshape(1, -1),
    )
    kv_a = lax.all_to_all(packed, "seq_1", 0, 0, tiled=True)
    swap = [(i, i ^ 1) for i in range(lax.axis_size("head"))]
    kv_b = lax.ppermute(kv_a, "head", swap)
    q_left = shift(queries, "seq_0", 1)
    q_right = shift(queries, "seq_0", -1)
    q_far = shift(queries, "seq_0", 2)

    b_map = lax.dynamic_slice_in_dim(state_in, column * STATE, STATE, 1)
    c_map = lax.dynamic_slice_in_dim(state_out, column * STATE, STATE, 1)
    send, running, run_t = call(
        local_kernel,
        [
            jax.ShapeDtypeStruct((ND, SLOT, 128), BF16),
            jax.ShapeDtypeStruct((TOK, HEADS), F32),
            jax.ShapeDtypeStruct((HEADS, TOK), F32),
        ],
        (
            place,
            ssm_input,
            step_size,
            b_map,
            decay_rate.reshape(1, -1),
            forget.reshape(1, -1),
            new_keys,
        ),
        "local",
        2 * TOK * COLS * STATE,
    )
    recv = lax.all_to_all(send, SEQ, 0, 0, tiled=True)
    base = call(
        within_kernel,
        jax.ShapeDtypeStruct((TOK, COLS), F32),
        (place, ssm_input, step_size, running, run_t, b_map, c_map, skip_gain.reshape(1, -1)),
        "within",
        4 * TOK * COLS * TOK,
    )
    back = call(
        scan_kernel,
        jax.ShapeDtypeStruct((ND, SLOT, 128), BF16),
        (place, recv),
        "scan",
        1000000,
    )
    carried = lax.all_to_all(back, SEQ, 0, 0, tiled=True)

    p_left, p_right, p_far = attend(
        place, (q_left, q_right, q_far), kv_a, kv_b, (-1, 1, 2), "attend_others"
    )
    (p_own,) = attend(place, (queries,), kv_a, kv_b, (0,), "attend_own")
    r_left = shift(p_left, "seq_0", -1)
    r_right = shift(p_right, "seq_0", 1)
    r_far = shift(p_far, "seq_0", 2)
    attended = call(
        merge_kernel,
        jax.ShapeDtypeStruct((TOK, QH * ATT_DIM), BF16),
        (place, p_own, r_left, r_right, r_far),
        "merge",
        1000000,
    )
    ssm_output, key_codes, key_scale = call(
        final_kernel,
        [
            jax.ShapeDtypeStruct((TOK, COLS), BF16),
            jax.ShapeDtypeStruct((TOK, KV_HEADS * ATT_DIM), BF16),
            jax.ShapeDtypeStruct((1, KV_HEADS * ATT_DIM), F32),
        ],
        (place, carried, base, c_map, running, new_keys),
        "final",
        2 * TOK * COLS * STATE,
        scratch=(pltpu.VMEM((STATE, COLS), BF16),),
    )
    return (ssm_output, attended, key_codes, key_scale.reshape(-1))


def solution(mesh):
    split = Mesh(mesh.devices.reshape(NX, NY, mesh.shape["head"]), ("seq_0", "seq_1", "head"))
    return jax.shard_map(
        body,
        mesh=split,
        in_specs=(
            P(SEQ, "head"),
            P(SEQ, None),
            P(SEQ, None),
            P(SEQ, "head"),
            P("head"),
            P(SEQ),
            P("head"),
            P(SEQ, "head"),
            P(SEQ, None),
            P(SEQ, None),
            P(SEQ, None),
            P(SEQ, None),
            P(),
            P(),
        ),
        out_specs=(P(SEQ, "head"), P(SEQ, "head"), P(SEQ, None), P()),
        check_vma=False,
    )
```

```python
import functools

import jax
import jax.numpy as jnp
from jax import lax
from jax.experimental import pallas as pl
from jax.experimental.pallas import tpu as pltpu
from jax.sharding import Mesh
from jax.sharding import PartitionSpec as P

SSM_HEADS = 256
HEAD_DIM = 64
STATE = 256
GROUPS = 8
ATT_HEADS = 64
KV_HEADS = 8
ATT_DIM = 128
SEQ = ("seq_0", "seq_1")
NX, NY, ND = 4, 8, 32

TOK = 192
CROWS = 64
NROWS = 96
HALF = CROWS + NROWS
HEADS = 16
COLS = HEADS * HEAD_DIM
QH = 4
ROWS = QH * TOK
STAT = 32
SENT = CROWS + NROWS + 16
SLOT = 72
BACK = 64
NEG = -1e30
LOG2E = 1.4426950408889634
SCALE = ATT_DIM**-0.5 * LOG2E
F32 = jnp.float32
BF16 = jnp.bfloat16
LIMIT = 24 << 20
HIGHEST = lax.Precision.HIGHEST


def whole():
    return pl.BlockSpec(memory_space=pltpu.VMEM)


def call(kernel, out_shape, args, name, flops, scratch=(), moved=1 << 21, after=()):
    def inner(*refs):
        kernel(*refs[: len(args)], *refs[len(args) + len(after) :])

    return pl.pallas_call(
        inner,
        out_shape=out_shape,
        in_specs=[pl.BlockSpec(memory_space=pltpu.SMEM)] + [whole()] * (len(args) - 1)
        + [whole()] * len(after),
        out_specs=jax.tree.map(lambda _: whole(), out_shape),
        scratch_shapes=list(scratch),
        compiler_params=pltpu.CompilerParams(vmem_limit_bytes=LIMIT),
        cost_estimate=pl.CostEstimate(flops=flops, bytes_accessed=moved, transcendentals=0),
        name=name,
    )(*args, *after)


def parts_of(value):
    hi = value.astype(BF16)
    left = value - hi.astype(F32)
    mid = left.astype(BF16)
    low = (left - mid.astype(F32)).astype(BF16)
    return hi, mid, low


def hold(value, after):
    return pl.pallas_call(
        lambda *refs: None,
        out_shape=jax.ShapeDtypeStruct(value.shape, value.dtype),
        in_specs=[pl.BlockSpec(memory_space=pl.ANY)] * (1 + len(after)),
        out_specs=pl.BlockSpec(memory_space=pl.ANY),
        input_output_aliases={0: 0},
        compiler_params=pltpu.CompilerParams(vmem_limit_bytes=LIMIT),
        name="hold",
    )(value, *after)


def spread_heads(per_head):
    rows = per_head.shape[0]
    low = lax.broadcasted_iota(jnp.int32, (rows, 128), 1) < HEAD_DIM
    tiles = []
    for j in range(HEADS // 2):
        tiles.append(
            jnp.where(low, per_head[:, 2 * j : 2 * j + 1], per_head[:, 2 * j + 1 : 2 * j + 2])
        )
    return jnp.concatenate(tiles, axis=1)


def pack_kernel(place, ck, cv, nk, nv, ks, vs, all_keys, out):
    keys = (ck[...].astype(F32) * ks[...]).astype(BF16)
    values = (cv[...].astype(F32) * vs[...]).astype(BF16)
    cache = jnp.concatenate([keys, values], axis=1)
    fresh = jnp.concatenate([nk[...], nv[...]], axis=1)
    peak = jnp.max(jnp.abs(all_keys[...].astype(F32)), axis=0, keepdims=True)
    lines = [peak[:, 256 * i : 256 * i + 256] for i in range(4)]
    lines.append(jnp.zeros((12, 256), F32))
    peaks = jnp.concatenate(lines, axis=0).astype(BF16)
    for k in range(NY):
        out[k, :CROWS, :] = cache
        out[k, CROWS:HALF, :] = fresh
        out[k, HALF:, :] = peaks


def pack(place, ck, cv, nk, nv, ks, vs):
    row = lambda i, p: (p[3], p[2])
    top = lambda i, p: (0, p[2])
    return pl.pallas_call(
        pack_kernel,
        out_shape=jax.ShapeDtypeStruct((NY, SENT, 2 * ATT_DIM), BF16),
        grid_spec=pltpu.PrefetchScalarGridSpec(
            num_scalar_prefetch=1,
            grid=(1,),
            in_specs=[
                pl.BlockSpec((CROWS, ATT_DIM), row),
                pl.BlockSpec((CROWS, ATT_DIM), row),
                pl.BlockSpec((NROWS, ATT_DIM), row),
                pl.BlockSpec((NROWS, ATT_DIM), row),
                pl.BlockSpec((1, ATT_DIM), top),
                pl.BlockSpec((1, ATT_DIM), top),
                pl.BlockSpec((TOK, KV_HEADS * ATT_DIM), lambda i, p: (0, 0)),
            ],
            out_specs=pl.BlockSpec((NY, SENT, 2 * ATT_DIM), lambda i, p: (0, 0, 0)),
        ),
        cost_estimate=pl.CostEstimate(flops=1000000, bytes_accessed=1 << 21, transcendentals=0),
        compiler_params=pltpu.CompilerParams(vmem_limit_bytes=58 << 20),
        name="pack",
    )(place, ck, cv, nk, nv, ks, vs, nk)


def local_kernel(place, x, step_t, b_map, rate_of, forget, send, run_out, run_t_out):
    rows = lax.broadcasted_iota(jnp.int32, (TOK, TOK), 0)
    cols = lax.broadcasted_iota(jnp.int32, (TOK, TOK), 1)
    square = lax.broadcasted_iota(jnp.int32, (HEADS, HEADS), 0) == lax.broadcasted_iota(
        jnp.int32, (HEADS, HEADS), 1
    )
    rate_col = jnp.sum(jnp.where(square, rate_of[...], 0.0), axis=1, keepdims=True)
    rate_t = -rate_col * step_t[...] - forget[...]
    run_t = jnp.dot(
        rate_t, (rows <= cols).astype(F32), precision=HIGHEST, preferred_element_type=F32
    )
    run_t_out[...] = run_t
    run_out[...] = run_t.T
    last = run_t[:, TOK - 1 : TOK]
    gain = spread_heads((jnp.exp(last - run_t) * step_t[...]).T)
    given = (x[...].astype(F32) * gain).astype(BF16)
    local = lax.dot_general(
        b_map[...], given, (((0,), (0,)), ((), ())), preferred_element_type=F32
    ).astype(BF16)
    final = jnp.sum(jnp.where(square, last, 0.0), axis=0, keepdims=True)
    decay = spread_heads(jnp.exp(jnp.broadcast_to(final, (8, HEADS))))[0:1, :]
    hi = decay.astype(BF16)
    low = (decay - hi.astype(F32)).astype(BF16)
    for d in range(ND):
        block, half = d // 2, d % 2
        tail = []
        for source in (hi, low):
            for j in range(4):
                at = (half * 4 + j) * 128
                tail.append(source[:, at : at + 128].astype(F32))
        for j in range(4):
            at = (half * 4 + j) * 128
            send[d, 16 * j : 16 * j + 16, :] = local[16 * block : 16 * block + 16, at : at + 128]
        send[d, BACK:, :] = jnp.concatenate(tail, axis=0).astype(BF16)


def within_kernel(place, x, step_t, running, run_t, b_map, c_map, skip, base):
    rows = lax.broadcasted_iota(jnp.int32, (TOK, TOK), 0)
    cols = lax.broadcasted_iota(jnp.int32, (TOK, TOK), 1)
    causal = rows >= cols
    gram = lax.dot_general(
        c_map[...], b_map[...], (((1,), (1,)), ((), ())), preferred_element_type=F32
    )
    signal = x[...].astype(F32)
    given = (signal * spread_heads(step_t[...].T)).astype(BF16)
    skips = spread_heads(jnp.broadcast_to(skip[...], (8, HEADS)))[0:1, :]
    low = lax.broadcasted_iota(jnp.int32, (TOK, 128), 1) < HEAD_DIM
    for j in range(HEADS // 2):
        sides = []
        part = given[:, 128 * j : 128 * j + 128]
        for h in (2 * j, 2 * j + 1):
            spread = running[:, h : h + 1] - run_t[h : h + 1, :]
            weight = jnp.exp(jnp.where(causal, spread, NEG)) * gram
            sides.append(jnp.dot(weight.astype(BF16), part, preferred_element_type=F32))
        at = slice(128 * j, 128 * j + 128)
        base[:, at] = jnp.where(low, sides[0], sides[1]) + skips[:, at] * signal[:, at]


def scan_kernel(place, recv, send):
    states = [jnp.zeros((16, 128), F32) for _ in range(4)]
    for s in range(ND):
        tail = recv[s, BACK:, :].astype(F32)
        for j in range(4):
            send[s, 16 * j : 16 * j + 16, :] = states[j].astype(BF16)
            decay = tail[j : j + 1, :] + tail[4 + j : 5 + j, :]
            states[j] = decay * states[j] + recv[s, 16 * j : 16 * j + 16, :].astype(F32)


def final_kernel(place, recv, base, c_map, running, out, carried):
    for d in range(ND):
        block, half = d // 2, d % 2
        for j in range(4):
            at = (half * 4 + j) * 128
            carried[16 * block : 16 * block + 16, at : at + 128] = recv[d, 16 * j : 16 * j + 16, :]
    prior = jnp.dot(c_map[...], carried[...], preferred_element_type=F32)
    out[...] = (base[...] + spread_heads(jnp.exp(running[...])) * prior).astype(BF16)


CACHED = 2 * NY * CROWS
FRESH = 2 * NY * NROWS
CHUNK = 256


def load_keys(pieces, keys, values):
    at = 0
    for first, count in ((0, CROWS), (CROWS, NROWS)):
        for ref in pieces:
            size = NY * count
            both = ref[:, first : first + count, :].reshape(size, 2 * ATT_DIM)
            keys[at : at + size, :] = both[:, :ATT_DIM]
            values[at : at + size, :ATT_DIM] = both[:, ATT_DIM:]
            at += size
    values[:, ATT_DIM:] = jnp.ones((NY * 2 * HALF, ATT_DIM), BF16)


def positions(place):
    col = lax.broadcasted_iota(jnp.int32, (1, FRESH), 1)
    base = jnp.zeros((1, FRESH), jnp.int32)
    for k in range(2 * NY):
        side = place[3] if k < NY else 1 - place[3]
        start = k % NY * TOK + side * NROWS - k * NROWS
        base = jnp.where(col >= k * NROWS, start, base)
    return col + base


def attend_kernel(own, place, *refs):
    count = 1 if own else NX - 1
    queries, pieces = refs[:count], refs[count : count + 2]
    outs = refs[count + 2 : 2 * count + 2]
    keys, values, q_rows, sums = refs[2 * count + 2 :]
    mine = place[0]
    load_keys(pieces, keys, values)
    for b in range(count):
        for h in range(QH):
            q_rows[b, h * TOK : (h + 1) * TOK, :] = queries[b][:, h * ATT_DIM : (h + 1) * ATT_DIM]

    def attend_block(b, last):
        q = q_rows[b]
        carry = None
        if own:
            pos = positions(place)
            row = lax.broadcasted_iota(jnp.int32, (TOK, 1), 0) + place[1] * TOK
            row = jnp.concatenate([row] * QH, axis=0)
        for at in range(0, last, CHUNK):
            scores = lax.dot_general(
                q, keys[at : at + CHUNK, :], (((1,), (1,)), ((), ())), preferred_element_type=F32
            )
            if own and at >= CACHED:
                seen = pos[:, at - CACHED : at - CACHED + CHUNK] <= row
                scores = jnp.where(seen, scores, NEG)
            best = jnp.max(jnp.maximum(scores[:, :128], scores[:, 128:]), axis=1, keepdims=True)
            top = best if carry is None else jnp.maximum(carry[1], best)
            probs = jnp.exp2(scores * SCALE - top * SCALE).astype(BF16)
            summed = jnp.dot(probs, values[at : at + CHUNK, :], preferred_element_type=F32)
            if carry is not None:
                summed += carry[0] * jnp.exp2((carry[1] - top) * SCALE)
            carry = (summed, top)
        summed, top = carry
        total = summed[:, ATT_DIM:]
        sums[b, :, :ATT_DIM] = summed[:, :ATT_DIM] / total
        sums[b, :, ATT_DIM:] = top * SCALE + jnp.log2(total)

    if own:
        attend_block(0, CACHED + FRESH)
    else:

        @pl.loop(0, count)
        def _(b):
            owner = lax.rem(mine + b + 1, NX)

            @pl.when(owner > mine)
            def _():
                attend_block(b, CACHED + FRESH)

            @pl.when(owner < mine)
            def _():
                attend_block(b, CACHED)

    peaks = jnp.max(pieces[0][:, HALF:, :].astype(F32), axis=0)
    peaks = jnp.concatenate(
        [peaks[r // 2 : r // 2 + 1, r % 2 * 128 : r % 2 * 128 + 128] for r in range(8)], axis=0
    )
    diagonal = lax.broadcasted_iota(jnp.int32, (128, 128), 0) == lax.broadcasted_iota(
        jnp.int32, (128, 128), 1
    )
    for b in range(count):
        outs[b][:ROWS, :] = sums[b, :, :ATT_DIM].astype(BF16)
        lines = []
        for k in range(ROWS // 128):
            part = sums[b, k * 128 : k * 128 + 128, ATT_DIM:]
            lines.append(jnp.sum(jnp.where(diagonal, part, 0.0), axis=0, keepdims=True))
        lines.append(jnp.zeros((2, ATT_DIM), F32))
        packed = [p.astype(F32) for p in parts_of(jnp.concatenate(lines, axis=0))]
        packed.append(peaks)
        outs[b][ROWS:, :] = jnp.concatenate(packed, axis=0).astype(BF16)


def attend(place, queries, pieces, name):
    count = len(queries)
    partial = jax.ShapeDtypeStruct((ROWS + STAT, ATT_DIM), BF16)
    return call(
        functools.partial(attend_kernel, count == 1),
        [partial] * count,
        (place, *queries, *pieces),
        name,
        count * 4 * ROWS * (CACHED + FRESH) * ATT_DIM,
        scratch=(
            pltpu.VMEM((CACHED + FRESH, ATT_DIM), BF16),
            pltpu.VMEM((CACHED + FRESH, 2 * ATT_DIM), BF16),
            pltpu.VMEM((count, ROWS, ATT_DIM), BF16),
            pltpu.VMEM((count, ROWS, 2 * ATT_DIM), F32),
        ),
    )


def merge_kernel(place, *refs):
    parts, nk, out, codes, scale = refs[:NX], *refs[NX:]
    peaks = functools.reduce(jnp.maximum, [ref[ROWS:, :].astype(F32)[24:32] for ref in parts])
    peaks = jnp.concatenate([peaks[r : r + 1, :] for r in range(8)], axis=1)
    key_scale = (peaks + 1e-6) / 127.0
    scale[...] = key_scale
    codes[...] = (nk[...].astype(F32) / key_scale).astype(BF16)
    diagonal = lax.broadcasted_iota(jnp.int32, (128, 128), 0) == lax.broadcasted_iota(
        jnp.int32, (128, 128), 1
    )
    stats = []
    for ref in parts:
        packed = ref[ROWS:, :].astype(F32)
        stats.append(packed[0:8] + packed[8:16] + packed[16:24])
    top = functools.reduce(jnp.maximum, stats)
    shares = [jnp.exp2(s - top) for s in stats]
    total = functools.reduce(jnp.add, shares)
    shares = [s / total for s in shares]
    pieces = []
    for k in range(ROWS // 128):
        summed = jnp.zeros((128, 128), F32)
        for share, ref in zip(shares, parts):
            line = jnp.where(diagonal, share[k : k + 1, :], 0.0)
            column = jnp.sum(line, axis=1, keepdims=True)
            summed += column * ref[k * 128 : k * 128 + 128, :].astype(F32)
        pieces.append(summed)
    result = jnp.concatenate(pieces, axis=0)
    for h in range(QH):
        out[:, h * ATT_DIM : (h + 1) * ATT_DIM] = result[h * TOK : (h + 1) * TOK, :].astype(BF16)


def shift(value, axis, by):
    size = lax.axis_size(axis)
    return lax.ppermute(value, axis, [(i, (i + by) % size) for i in range(size)])


def body(
    ssm_input,
    state_in,
    state_out,
    step_size,
    decay_rate,
    forget,
    skip_gain,
    queries,
    new_keys,
    new_values,
    cache_keys,
    cache_values,
    cache_key_scale,
    cache_value_scale,
):
    head = lax.axis_index("head")
    step_t = step_size.T
    column, core = head // 2, head % 2
    place = jnp.stack(
        [lax.axis_index("seq_0"), lax.axis_index("seq_1"), column, core]
    ).astype(jnp.int32)

    packed = pack(
        place,
        cache_keys,
        cache_values,
        new_keys,
        new_values,
        cache_key_scale.reshape(1, -1),
        cache_value_scale.reshape(1, -1),
    )
    swap = [(i, i ^ 1) for i in range(lax.axis_size("head"))]
    kv_a = lax.all_to_all(packed, "seq_1", 0, 0, tiled=True)
    q_left = shift(queries, "seq_0", 1)
    q_right = shift(queries, "seq_0", -1)
    q_far = shift(queries, "seq_0", 2)

    b_map = lax.dynamic_slice_in_dim(state_in, column * STATE, STATE, 1)
    c_map = lax.dynamic_slice_in_dim(state_out, column * STATE, STATE, 1)
    send, running, run_t = call(
        local_kernel,
        [
            jax.ShapeDtypeStruct((ND, SLOT, 128), BF16),
            jax.ShapeDtypeStruct((TOK, HEADS), F32),
            jax.ShapeDtypeStruct((HEADS, TOK), F32),
        ],
        (
            place,
            ssm_input,
            step_t,
            b_map,
            decay_rate.reshape(1, -1),
            forget.reshape(1, -1),
        ),
        "local",
        2 * TOK * COLS * STATE,
        after=(packed,),
    )
    kv_a = hold(kv_a, (run_t, q_left, q_right, q_far))
    kv_b = lax.ppermute(kv_a, "head", swap)
    pieces = (kv_a, kv_b)
    send = hold(send, (kv_b,))
    recv = lax.all_to_all(send, SEQ, 0, 0, tiled=True)
    base = call(
        within_kernel,
        jax.ShapeDtypeStruct((TOK, COLS), F32),
        (place, ssm_input, step_t, running, run_t, b_map, c_map, skip_gain.reshape(1, -1)),
        "within",
        4 * TOK * COLS * TOK,
    )
    p_right, p_far, p_left = attend(
        place, (q_right, q_far, q_left), pieces, "attend_others"
    )
    (p_own,) = attend(place, (queries,), pieces, "attend_own")
    back = call(
        scan_kernel,
        jax.ShapeDtypeStruct((ND, BACK, 128), BF16),
        (place, recv),
        "scan",
        1000000,
        after=(base, p_right),
    )
    carried = lax.all_to_all(back, SEQ, 0, 0, tiled=True)

    r_left = shift(p_left, "seq_0", -1)
    r_right = shift(p_right, "seq_0", 1)
    r_far = shift(p_far, "seq_0", 2)
    attended, key_codes, key_scale = call(
        merge_kernel,
        [
            jax.ShapeDtypeStruct((TOK, QH * ATT_DIM), BF16),
            jax.ShapeDtypeStruct((TOK, KV_HEADS * ATT_DIM), BF16),
            jax.ShapeDtypeStruct((1, KV_HEADS * ATT_DIM), F32),
        ],
        (place, p_own, r_left, r_right, r_far, new_keys),
        "merge",
        1000000,
    )
    ssm_output = call(
        final_kernel,
        jax.ShapeDtypeStruct((TOK, COLS), BF16),
        (place, carried, base, c_map, running),
        "final",
        2 * TOK * COLS * STATE,
        scratch=(pltpu.VMEM((STATE, COLS), BF16),),
    )
    return (ssm_output, attended, key_codes, key_scale.reshape(-1))


def solution(mesh):
    split = Mesh(mesh.devices.reshape(NX, NY, mesh.shape["head"]), ("seq_0", "seq_1", "head"))
    return jax.shard_map(
        body,
        mesh=split,
        in_specs=(
            P(SEQ, "head"),
            P(SEQ, None),
            P(SEQ, None),
            P(SEQ, "head"),
            P("head"),
            P(SEQ),
            P("head"),
            P(SEQ, "head"),
            P(SEQ, None),
            P(SEQ, None),
            P(SEQ, None),
            P(SEQ, None),
            P(),
            P(),
        ),
        out_specs=(P(SEQ, "head"), P(SEQ, "head"), P(SEQ, None), P()),
        check_vma=False,
    )
```

```python
import functools

import jax
import jax.numpy as jnp
from jax import lax
from jax.experimental import pallas as pl
from jax.experimental.pallas import tpu as pltpu
from jax.sharding import Mesh
from jax.sharding import PartitionSpec as P

SSM_HEADS = 256
HEAD_DIM = 64
STATE = 256
GROUPS = 8
ATT_HEADS = 64
KV_HEADS = 8
ATT_DIM = 128
SEQ = ("seq_0", "seq_1")
NX, NY, ND = 4, 8, 32

TOK = 192
CROWS = 64
NROWS = 96
HALF = CROWS + NROWS
HEADS = 16
COLS = HEADS * HEAD_DIM
QH = 4
ROWS = QH * TOK
STAT = 32
SENT = CROWS + NROWS + 16
SLOT = 72
BACK = 64
NEG = -1e30
LOG2E = 1.4426950408889634
SCALE = ATT_DIM**-0.5 * LOG2E
F32 = jnp.float32
BF16 = jnp.bfloat16
LIMIT = 24 << 20
HIGHEST = lax.Precision.HIGHEST


def whole():
    return pl.BlockSpec(memory_space=pltpu.VMEM)


def call(kernel, out_shape, args, name, flops, scratch=(), moved=1 << 21, after=()):
    def inner(*refs):
        kernel(*refs[: len(args)], *refs[len(args) + len(after) :])

    return pl.pallas_call(
        inner,
        out_shape=out_shape,
        in_specs=[pl.BlockSpec(memory_space=pltpu.SMEM)] + [whole()] * (len(args) - 1)
        + [whole()] * len(after),
        out_specs=jax.tree.map(lambda _: whole(), out_shape),
        scratch_shapes=list(scratch),
        compiler_params=pltpu.CompilerParams(vmem_limit_bytes=LIMIT),
        cost_estimate=pl.CostEstimate(flops=flops, bytes_accessed=moved, transcendentals=0),
        name=name,
    )(*args, *after)


def parts_of(value):
    hi = value.astype(BF16)
    left = value - hi.astype(F32)
    mid = left.astype(BF16)
    low = (left - mid.astype(F32)).astype(BF16)
    return hi, mid, low


def hold(value, after):
    return pl.pallas_call(
        lambda *refs: None,
        out_shape=jax.ShapeDtypeStruct(value.shape, value.dtype),
        in_specs=[pl.BlockSpec(memory_space=pl.ANY)] * (1 + len(after)),
        out_specs=pl.BlockSpec(memory_space=pl.ANY),
        input_output_aliases={0: 0},
        compiler_params=pltpu.CompilerParams(vmem_limit_bytes=LIMIT),
        name="hold",
    )(value, *after)


def spread_heads(per_head):
    rows = per_head.shape[0]
    low = lax.broadcasted_iota(jnp.int32, (rows, 128), 1) < HEAD_DIM
    tiles = []
    for j in range(HEADS // 2):
        tiles.append(
            jnp.where(low, per_head[:, 2 * j : 2 * j + 1], per_head[:, 2 * j + 1 : 2 * j + 2])
        )
    return jnp.concatenate(tiles, axis=1)


def pack_kernel(place, ck, cv, nk, nv, ks, vs, all_keys, out):
    keys = (ck[...].astype(F32) * ks[...]).astype(BF16)
    values = (cv[...].astype(F32) * vs[...]).astype(BF16)
    cache = jnp.concatenate([keys, values], axis=1)
    fresh = jnp.concatenate([nk[...], nv[...]], axis=1)
    peak = jnp.max(jnp.abs(all_keys[...].astype(F32)), axis=0, keepdims=True)
    lines = [peak[:, 256 * i : 256 * i + 256] for i in range(4)]
    lines.append(jnp.zeros((12, 256), F32))
    peaks = jnp.concatenate(lines, axis=0).astype(BF16)
    for k in range(NY):
        out[k, :CROWS, :] = cache
        out[k, CROWS:HALF, :] = fresh
        out[k, HALF:, :] = peaks


def pack(place, ck, cv, nk, nv, ks, vs):
    row = lambda i, p: (p[3], p[2])
    top = lambda i, p: (0, p[2])
    return pl.pallas_call(
        pack_kernel,
        out_shape=jax.ShapeDtypeStruct((NY, SENT, 2 * ATT_DIM), BF16),
        grid_spec=pltpu.PrefetchScalarGridSpec(
            num_scalar_prefetch=1,
            grid=(1,),
            in_specs=[
                pl.BlockSpec((CROWS, ATT_DIM), row),
                pl.BlockSpec((CROWS, ATT_DIM), row),
                pl.BlockSpec((NROWS, ATT_DIM), row),
                pl.BlockSpec((NROWS, ATT_DIM), row),
                pl.BlockSpec((1, ATT_DIM), top),
                pl.BlockSpec((1, ATT_DIM), top),
                pl.BlockSpec((TOK, KV_HEADS * ATT_DIM), lambda i, p: (0, 0)),
            ],
            out_specs=pl.BlockSpec((NY, SENT, 2 * ATT_DIM), lambda i, p: (0, 0, 0)),
        ),
        cost_estimate=pl.CostEstimate(flops=1000000, bytes_accessed=1 << 21, transcendentals=0),
        compiler_params=pltpu.CompilerParams(vmem_limit_bytes=58 << 20),
        name="pack",
    )(place, ck, cv, nk, nv, ks, vs, nk)


def local_kernel(place, x, step_t, b_map, rate_of, forget, send, run_out, run_t_out):
    rows = lax.broadcasted_iota(jnp.int32, (TOK, TOK), 0)
    cols = lax.broadcasted_iota(jnp.int32, (TOK, TOK), 1)
    square = lax.broadcasted_iota(jnp.int32, (HEADS, HEADS), 0) == lax.broadcasted_iota(
        jnp.int32, (HEADS, HEADS), 1
    )
    rate_col = jnp.sum(jnp.where(square, rate_of[...], 0.0), axis=1, keepdims=True)
    rate_t = -rate_col * step_t[...] - forget[...]
    run_t = jnp.dot(
        rate_t, (rows <= cols).astype(F32), precision=HIGHEST, preferred_element_type=F32
    )
    run_t_out[...] = run_t
    run_out[...] = run_t.T
    last = run_t[:, TOK - 1 : TOK]
    gain = spread_heads((jnp.exp(last - run_t) * step_t[...]).T)
    given = (x[...].astype(F32) * gain).astype(BF16)
    local = lax.dot_general(
        b_map[...], given, (((0,), (0,)), ((), ())), preferred_element_type=F32
    ).astype(BF16)
    final = jnp.sum(jnp.where(square, last, 0.0), axis=0, keepdims=True)
    decay = spread_heads(jnp.exp(jnp.broadcast_to(final, (8, HEADS))))[0:1, :]
    hi = decay.astype(BF16)
    low = (decay - hi.astype(F32)).astype(BF16)
    for d in range(ND):
        block, half = d // 2, d % 2
        tail = []
        for source in (hi, low):
            for j in range(4):
                at = (half * 4 + j) * 128
                tail.append(source[:, at : at + 128].astype(F32))
        for j in range(4):
            at = (half * 4 + j) * 128
            send[d, 16 * j : 16 * j + 16, :] = local[16 * block : 16 * block + 16, at : at + 128]
        send[d, BACK:, :] = jnp.concatenate(tail, axis=0).astype(BF16)


def within_kernel(place, x, step_t, running, run_t, b_map, c_map, skip, base):
    rows = lax.broadcasted_iota(jnp.int32, (TOK, TOK), 0)
    cols = lax.broadcasted_iota(jnp.int32, (TOK, TOK), 1)
    causal = rows >= cols
    gram = lax.dot_general(
        c_map[...], b_map[...], (((1,), (1,)), ((), ())), preferred_element_type=F32
    )
    signal = x[...].astype(F32)
    given = (signal * spread_heads(step_t[...].T)).astype(BF16)
    skips = spread_heads(jnp.broadcast_to(skip[...], (8, HEADS)))[0:1, :]
    low = lax.broadcasted_iota(jnp.int32, (TOK, 128), 1) < HEAD_DIM
    for j in range(HEADS // 2):
        sides = []
        part = given[:, 128 * j : 128 * j + 128]
        for h in (2 * j, 2 * j + 1):
            spread = running[:, h : h + 1] - run_t[h : h + 1, :]
            weight = jnp.exp(jnp.where(causal, spread, NEG)) * gram
            sides.append(jnp.dot(weight.astype(BF16), part, preferred_element_type=F32))
        at = slice(128 * j, 128 * j + 128)
        base[:, at] = jnp.where(low, sides[0], sides[1]) + skips[:, at] * signal[:, at]


def scan_kernel(place, recv, send):
    states = [jnp.zeros((16, 128), F32) for _ in range(4)]
    for s in range(ND):
        tail = recv[s, BACK:, :].astype(F32)
        for j in range(4):
            send[s, 16 * j : 16 * j + 16, :] = states[j].astype(BF16)
            decay = tail[j : j + 1, :] + tail[4 + j : 5 + j, :]
            states[j] = decay * states[j] + recv[s, 16 * j : 16 * j + 16, :].astype(F32)


def final_kernel(place, recv, base, c_map, running, out, carried):
    for d in range(ND):
        block, half = d // 2, d % 2
        for j in range(4):
            at = (half * 4 + j) * 128
            carried[16 * block : 16 * block + 16, at : at + 128] = recv[d, 16 * j : 16 * j + 16, :]
    prior = jnp.dot(c_map[...], carried[...], preferred_element_type=F32)
    out[...] = (base[...] + spread_heads(jnp.exp(running[...])) * prior).astype(BF16)


CACHED = 2 * NY * CROWS
FRESH = 2 * NY * NROWS
CHUNK = 256


def load_keys(pieces, keys, values):
    at = 0
    for first, count in ((0, CROWS), (CROWS, NROWS)):
        for ref in pieces:
            size = NY * count
            both = ref[:, first : first + count, :].reshape(size, 2 * ATT_DIM)
            keys[at : at + size, :] = both[:, :ATT_DIM]
            values[at : at + size, :ATT_DIM] = both[:, ATT_DIM:]
            at += size
    values[:, ATT_DIM:] = jnp.ones((NY * 2 * HALF, ATT_DIM), BF16)


def positions(place):
    col = lax.broadcasted_iota(jnp.int32, (1, FRESH), 1)
    base = jnp.zeros((1, FRESH), jnp.int32)
    for k in range(2 * NY):
        side = place[3] if k < NY else 1 - place[3]
        start = k % NY * TOK + side * NROWS - k * NROWS
        base = jnp.where(col >= k * NROWS, start, base)
    return col + base


def attend_kernel(own, place, *refs):
    count = 1 if own else NX - 1
    queries, pieces = refs[:count], refs[count : count + 2]
    outs = refs[count + 2 : 2 * count + 2]
    keys, values, q_rows, sums = refs[2 * count + 2 :]
    mine = place[0]
    load_keys(pieces, keys, values)
    for b in range(count):
        for h in range(QH):
            q_rows[b, h * TOK : (h + 1) * TOK, :] = queries[b][:, h * ATT_DIM : (h + 1) * ATT_DIM]

    def attend_block(b, last):
        q = q_rows[b]
        carry = None
        if own:
            pos = positions(place)
            row = lax.broadcasted_iota(jnp.int32, (TOK, 1), 0) + place[1] * TOK
            row = jnp.concatenate([row] * QH, axis=0)
        for at in range(0, last, CHUNK):
            scores = lax.dot_general(
                q, keys[at : at + CHUNK, :], (((1,), (1,)), ((), ())), preferred_element_type=F32
            )
            if own and at >= CACHED:
                seen = pos[:, at - CACHED : at - CACHED + CHUNK] <= row
                scores = jnp.where(seen, scores, NEG)
            best = jnp.max(jnp.maximum(scores[:, :128], scores[:, 128:]), axis=1, keepdims=True)
            top = best if carry is None else jnp.maximum(carry[1], best)
            probs = jnp.exp2(scores * SCALE - top * SCALE).astype(BF16)
            summed = jnp.dot(probs, values[at : at + CHUNK, :], preferred_element_type=F32)
            if carry is not None:
                summed += carry[0] * jnp.exp2((carry[1] - top) * SCALE)
            carry = (summed, top)
        summed, top = carry
        total = summed[:, ATT_DIM:]
        sums[b, :, :ATT_DIM] = summed[:, :ATT_DIM] / total
        sums[b, :, ATT_DIM:] = top * SCALE + jnp.log2(total)

    if own:
        attend_block(0, CACHED + FRESH)
    else:

        @pl.loop(0, count)
        def _(b):
            owner = lax.rem(mine + b + 1, NX)

            @pl.when(owner > mine)
            def _():
                attend_block(b, CACHED + FRESH)

            @pl.when(owner < mine)
            def _():
                attend_block(b, CACHED)

    peaks = jnp.max(pieces[0][:, HALF:, :].astype(F32), axis=0)
    peaks = jnp.concatenate(
        [peaks[r // 2 : r // 2 + 1, r % 2 * 128 : r % 2 * 128 + 128] for r in range(8)], axis=0
    )
    diagonal = lax.broadcasted_iota(jnp.int32, (128, 128), 0) == lax.broadcasted_iota(
        jnp.int32, (128, 128), 1
    )
    for b in range(count):
        outs[b][:ROWS, :] = sums[b, :, :ATT_DIM].astype(BF16)
        lines = []
        for k in range(ROWS // 128):
            part = sums[b, k * 128 : k * 128 + 128, ATT_DIM:]
            lines.append(jnp.sum(jnp.where(diagonal, part, 0.0), axis=0, keepdims=True))
        lines.append(jnp.zeros((2, ATT_DIM), F32))
        packed = [p.astype(F32) for p in parts_of(jnp.concatenate(lines, axis=0))]
        packed.append(peaks)
        outs[b][ROWS:, :] = jnp.concatenate(packed, axis=0).astype(BF16)


def attend(place, queries, pieces, name):
    count = len(queries)
    partial = jax.ShapeDtypeStruct((ROWS + STAT, ATT_DIM), BF16)
    return call(
        functools.partial(attend_kernel, count == 1),
        [partial] * count,
        (place, *queries, *pieces),
        name,
        60_000_000_000 if count > 1 else 4 * ROWS * (CACHED + FRESH) * ATT_DIM,
        scratch=(
            pltpu.VMEM((CACHED + FRESH, ATT_DIM), BF16),
            pltpu.VMEM((CACHED + FRESH, 2 * ATT_DIM), BF16),
            pltpu.VMEM((count, ROWS, ATT_DIM), BF16),
            pltpu.VMEM((count, ROWS, 2 * ATT_DIM), F32),
        ),
    )


def merge_kernel(place, *refs):
    parts, nk, out, codes, scale = refs[:NX], *refs[NX:]
    peaks = functools.reduce(jnp.maximum, [ref[ROWS:, :].astype(F32)[24:32] for ref in parts])
    peaks = jnp.concatenate([peaks[r : r + 1, :] for r in range(8)], axis=1)
    key_scale = (peaks + 1e-6) / 127.0
    scale[...] = key_scale
    codes[...] = (nk[...].astype(F32) / key_scale).astype(BF16)
    diagonal = lax.broadcasted_iota(jnp.int32, (128, 128), 0) == lax.broadcasted_iota(
        jnp.int32, (128, 128), 1
    )
    stats = []
    for ref in parts:
        packed = ref[ROWS:, :].astype(F32)
        stats.append(packed[0:8] + packed[8:16] + packed[16:24])
    top = functools.reduce(jnp.maximum, stats)
    shares = [jnp.exp2(s - top) for s in stats]
    total = functools.reduce(jnp.add, shares)
    shares = [s / total for s in shares]
    pieces = []
    for k in range(ROWS // 128):
        summed = jnp.zeros((128, 128), F32)
        for share, ref in zip(shares, parts):
            line = jnp.where(diagonal, share[k : k + 1, :], 0.0)
            column = jnp.sum(line, axis=1, keepdims=True)
            summed += column * ref[k * 128 : k * 128 + 128, :].astype(F32)
        pieces.append(summed)
    result = jnp.concatenate(pieces, axis=0)
    for h in range(QH):
        out[:, h * ATT_DIM : (h + 1) * ATT_DIM] = result[h * TOK : (h + 1) * TOK, :].astype(BF16)


def shift(value, axis, by):
    size = lax.axis_size(axis)
    return lax.ppermute(value, axis, [(i, (i + by) % size) for i in range(size)])


def body(
    ssm_input,
    state_in,
    state_out,
    step_size,
    decay_rate,
    forget,
    skip_gain,
    queries,
    new_keys,
    new_values,
    cache_keys,
    cache_values,
    cache_key_scale,
    cache_value_scale,
):
    head = lax.axis_index("head")
    step_t = step_size.T
    column, core = head // 2, head % 2
    place = jnp.stack(
        [lax.axis_index("seq_0"), lax.axis_index("seq_1"), column, core]
    ).astype(jnp.int32)

    packed = pack(
        place,
        cache_keys,
        cache_values,
        new_keys,
        new_values,
        cache_key_scale.reshape(1, -1),
        cache_value_scale.reshape(1, -1),
    )
    swap = [(i, i ^ 1) for i in range(lax.axis_size("head"))]
    kv_a = lax.all_to_all(packed, "seq_1", 0, 0, tiled=True)
    q_left = shift(queries, "seq_0", 1)
    q_right = shift(queries, "seq_0", -1)
    q_far = shift(queries, "seq_0", 2)

    b_map = lax.dynamic_slice_in_dim(state_in, column * STATE, STATE, 1)
    c_map = lax.dynamic_slice_in_dim(state_out, column * STATE, STATE, 1)
    send, running, run_t = call(
        local_kernel,
        [
            jax.ShapeDtypeStruct((ND, SLOT, 128), BF16),
            jax.ShapeDtypeStruct((TOK, HEADS), F32),
            jax.ShapeDtypeStruct((HEADS, TOK), F32),
        ],
        (
            place,
            ssm_input,
            step_t,
            b_map,
            decay_rate.reshape(1, -1),
            forget.reshape(1, -1),
        ),
        "local",
        2 * TOK * COLS * STATE,
        after=(packed,),
    )
    kv_a = hold(kv_a, (run_t, q_left, q_right, q_far))
    kv_b = lax.ppermute(kv_a, "head", swap)
    pieces = (kv_a, kv_b)
    send = hold(send, (kv_a,))
    recv = lax.all_to_all(send, SEQ, 0, 0, tiled=True)
    p_right, p_far, p_left = attend(
        place, (q_right, q_far, q_left), pieces, "attend_others"
    )
    (p_own,) = attend(place, (queries,), pieces, "attend_own")
    base = call(
        within_kernel,
        jax.ShapeDtypeStruct((TOK, COLS), F32),
        (place, ssm_input, step_t, running, run_t, b_map, c_map, skip_gain.reshape(1, -1)),
        "within",
        4 * TOK * COLS * TOK,
        after=(p_right,),
    )
    back = call(
        scan_kernel,
        jax.ShapeDtypeStruct((ND, BACK, 128), BF16),
        (place, recv),
        "scan",
        1000000,
        after=(base, p_left),
    )
    carried = lax.all_to_all(back, SEQ, 0, 0, tiled=True)

    r_left = shift(p_left, "seq_0", -1)
    r_right = shift(p_right, "seq_0", 1)
    r_far = shift(p_far, "seq_0", 2)
    attended, key_codes, key_scale = call(
        merge_kernel,
        [
            jax.ShapeDtypeStruct((TOK, QH * ATT_DIM), BF16),
            jax.ShapeDtypeStruct((TOK, KV_HEADS * ATT_DIM), BF16),
            jax.ShapeDtypeStruct((1, KV_HEADS * ATT_DIM), F32),
        ],
        (place, p_own, r_left, r_right, r_far, new_keys),
        "merge",
        1000000,
    )
    ssm_output = call(
        final_kernel,
        jax.ShapeDtypeStruct((TOK, COLS), BF16),
        (place, carried, base, c_map, running),
        "final",
        2 * TOK * COLS * STATE,
        scratch=(pltpu.VMEM((STATE, COLS), BF16),),
    )
    return (ssm_output, attended, key_codes, key_scale.reshape(-1))


def solution(mesh):
    split = Mesh(mesh.devices.reshape(NX, NY, mesh.shape["head"]), ("seq_0", "seq_1", "head"))
    return jax.shard_map(
        body,
        mesh=split,
        in_specs=(
            P(SEQ, "head"),
            P(SEQ, None),
            P(SEQ, None),
            P(SEQ, "head"),
            P("head"),
            P(SEQ),
            P("head"),
            P(SEQ, "head"),
            P(SEQ, None),
            P(SEQ, None),
            P(SEQ, None),
            P(SEQ, None),
            P(),
            P(),
        ),
        out_specs=(P(SEQ, "head"), P(SEQ, "head"), P(SEQ, None), P()),
        check_vma=False,
    )
```

```python
import functools

import jax
import jax.numpy as jnp
from jax import lax
from jax.experimental import pallas as pl
from jax.experimental.pallas import tpu as pltpu
from jax.sharding import Mesh
from jax.sharding import PartitionSpec as P

SSM_HEADS = 256
HEAD_DIM = 64
STATE = 256
GROUPS = 8
ATT_HEADS = 64
KV_HEADS = 8
ATT_DIM = 128
SEQ = ("seq_0", "seq_1")
NX, NY, ND = 4, 8, 32

TOK = 192
CROWS = 64
NROWS = 96
HALF = CROWS + NROWS
HEADS = 16
COLS = HEADS * HEAD_DIM
QH = 4
ROWS = QH * TOK
STAT = 32
SENT = CROWS + NROWS + 16
SLOT = 72
BACK = 64
NEG = -1e30
LOG2E = 1.4426950408889634
SCALE = ATT_DIM**-0.5 * LOG2E
F32 = jnp.float32
BF16 = jnp.bfloat16
LIMIT = 24 << 20
HIGHEST = lax.Precision.HIGHEST


def whole():
    return pl.BlockSpec(memory_space=pltpu.VMEM)


def call(kernel, out_shape, args, name, flops, scratch=(), moved=1 << 21, after=()):
    def inner(*refs):
        kernel(*refs[: len(args)], *refs[len(args) + len(after) :])

    return pl.pallas_call(
        inner,
        out_shape=out_shape,
        in_specs=[pl.BlockSpec(memory_space=pltpu.SMEM)] + [whole()] * (len(args) - 1)
        + [whole()] * len(after),
        out_specs=jax.tree.map(lambda _: whole(), out_shape),
        scratch_shapes=list(scratch),
        compiler_params=pltpu.CompilerParams(vmem_limit_bytes=LIMIT),
        cost_estimate=pl.CostEstimate(flops=flops, bytes_accessed=moved, transcendentals=0),
        name=name,
    )(*args, *after)


def parts_of(value):
    hi = value.astype(BF16)
    left = value - hi.astype(F32)
    mid = left.astype(BF16)
    low = (left - mid.astype(F32)).astype(BF16)
    return hi, mid, low


def hold(value, after):
    return pl.pallas_call(
        lambda *refs: None,
        out_shape=jax.ShapeDtypeStruct(value.shape, value.dtype),
        in_specs=[pl.BlockSpec(memory_space=pl.ANY)] * (1 + len(after)),
        out_specs=pl.BlockSpec(memory_space=pl.ANY),
        input_output_aliases={0: 0},
        compiler_params=pltpu.CompilerParams(vmem_limit_bytes=LIMIT),
        name="hold",
    )(value, *after)


def spread_heads(per_head):
    rows = per_head.shape[0]
    low = lax.broadcasted_iota(jnp.int32, (rows, 128), 1) < HEAD_DIM
    tiles = []
    for j in range(HEADS // 2):
        tiles.append(
            jnp.where(low, per_head[:, 2 * j : 2 * j + 1], per_head[:, 2 * j + 1 : 2 * j + 2])
        )
    return jnp.concatenate(tiles, axis=1)


def pack_kernel(place, ck, cv, nk, nv, ks, vs, all_keys, out):
    keys = (ck[...].astype(F32) * ks[...]).astype(BF16)
    values = (cv[...].astype(F32) * vs[...]).astype(BF16)
    cache = jnp.concatenate([keys, values], axis=1)
    fresh = jnp.concatenate([nk[...], nv[...]], axis=1)
    peak = jnp.max(jnp.abs(all_keys[...].astype(F32)), axis=0, keepdims=True)
    lines = [peak[:, 256 * i : 256 * i + 256] for i in range(4)]
    lines.append(jnp.zeros((12, 256), F32))
    peaks = jnp.concatenate(lines, axis=0).astype(BF16)
    for k in range(NY):
        out[k, :CROWS, :] = cache
        out[k, CROWS:HALF, :] = fresh
        out[k, HALF:, :] = peaks


def pack(place, ck, cv, nk, nv, ks, vs):
    row = lambda i, p: (p[3], p[2])
    top = lambda i, p: (0, p[2])
    return pl.pallas_call(
        pack_kernel,
        out_shape=jax.ShapeDtypeStruct((NY, SENT, 2 * ATT_DIM), BF16),
        grid_spec=pltpu.PrefetchScalarGridSpec(
            num_scalar_prefetch=1,
            grid=(1,),
            in_specs=[
                pl.BlockSpec((CROWS, ATT_DIM), row),
                pl.BlockSpec((CROWS, ATT_DIM), row),
                pl.BlockSpec((NROWS, ATT_DIM), row),
                pl.BlockSpec((NROWS, ATT_DIM), row),
                pl.BlockSpec((1, ATT_DIM), top),
                pl.BlockSpec((1, ATT_DIM), top),
                pl.BlockSpec((TOK, KV_HEADS * ATT_DIM), lambda i, p: (0, 0)),
            ],
            out_specs=pl.BlockSpec((NY, SENT, 2 * ATT_DIM), lambda i, p: (0, 0, 0)),
        ),
        cost_estimate=pl.CostEstimate(flops=1000000, bytes_accessed=1 << 21, transcendentals=0),
        compiler_params=pltpu.CompilerParams(vmem_limit_bytes=58 << 20),
        name="pack",
    )(place, ck, cv, nk, nv, ks, vs, nk)


def local_kernel(place, x, step_t, b_map, rate_of, forget, send, run_out, run_t_out):
    rows = lax.broadcasted_iota(jnp.int32, (TOK, TOK), 0)
    cols = lax.broadcasted_iota(jnp.int32, (TOK, TOK), 1)
    square = lax.broadcasted_iota(jnp.int32, (HEADS, HEADS), 0) == lax.broadcasted_iota(
        jnp.int32, (HEADS, HEADS), 1
    )
    rate_col = jnp.sum(jnp.where(square, rate_of[...], 0.0), axis=1, keepdims=True)
    rate_t = -rate_col * step_t[...] - forget[...]
    run_t = jnp.dot(
        rate_t, (rows <= cols).astype(F32), precision=HIGHEST, preferred_element_type=F32
    )
    run_t_out[...] = run_t
    run_out[...] = run_t.T
    last = run_t[:, TOK - 1 : TOK]
    gain = spread_heads((jnp.exp(last - run_t) * step_t[...]).T)
    given = (x[...].astype(F32) * gain).astype(BF16)
    local = lax.dot_general(
        b_map[...], given, (((0,), (0,)), ((), ())), preferred_element_type=F32
    ).astype(BF16)
    final = jnp.sum(jnp.where(square, last, 0.0), axis=0, keepdims=True)
    decay = spread_heads(jnp.exp(jnp.broadcast_to(final, (8, HEADS))))[0:1, :]
    hi = decay.astype(BF16)
    low = (decay - hi.astype(F32)).astype(BF16)
    for d in range(ND):
        block, half = d // 2, d % 2
        tail = []
        for source in (hi, low):
            for j in range(4):
                at = (half * 4 + j) * 128
                tail.append(source[:, at : at + 128].astype(F32))
        for j in range(4):
            at = (half * 4 + j) * 128
            send[d, 16 * j : 16 * j + 16, :] = local[16 * block : 16 * block + 16, at : at + 128]
        send[d, BACK:, :] = jnp.concatenate(tail, axis=0).astype(BF16)


def within_kernel(place, x, step_t, running, run_t, b_map, c_map, skip, base):
    rows = lax.broadcasted_iota(jnp.int32, (TOK, TOK), 0)
    cols = lax.broadcasted_iota(jnp.int32, (TOK, TOK), 1)
    causal = rows >= cols
    gram = lax.dot_general(
        c_map[...], b_map[...], (((1,), (1,)), ((), ())), preferred_element_type=F32
    )
    signal = x[...].astype(F32)
    given = (signal * spread_heads(step_t[...].T)).astype(BF16)
    skips = spread_heads(jnp.broadcast_to(skip[...], (8, HEADS)))[0:1, :]
    low = lax.broadcasted_iota(jnp.int32, (TOK, 128), 1) < HEAD_DIM
    for j in range(HEADS // 2):
        sides = []
        part = given[:, 128 * j : 128 * j + 128]
        for h in (2 * j, 2 * j + 1):
            spread = running[:, h : h + 1] - run_t[h : h + 1, :]
            weight = jnp.exp(jnp.where(causal, spread, NEG)) * gram
            sides.append(jnp.dot(weight.astype(BF16), part, preferred_element_type=F32))
        at = slice(128 * j, 128 * j + 128)
        base[:, at] = jnp.where(low, sides[0], sides[1]) + skips[:, at] * signal[:, at]


def scan_kernel(place, recv, send):
    states = [jnp.zeros((16, 128), F32) for _ in range(4)]
    for s in range(ND):
        tail = recv[s, BACK:, :].astype(F32)
        for j in range(4):
            send[s, 16 * j : 16 * j + 16, :] = states[j].astype(BF16)
            decay = tail[j : j + 1, :] + tail[4 + j : 5 + j, :]
            states[j] = decay * states[j] + recv[s, 16 * j : 16 * j + 16, :].astype(F32)


def final_kernel(place, recv, base, c_map, running, out, carried):
    for d in range(ND):
        block, half = d // 2, d % 2
        for j in range(4):
            at = (half * 4 + j) * 128
            carried[16 * block : 16 * block + 16, at : at + 128] = recv[d, 16 * j : 16 * j + 16, :]
    prior = jnp.dot(c_map[...], carried[...], preferred_element_type=F32)
    out[...] = (base[...] + spread_heads(jnp.exp(running[...])) * prior).astype(BF16)


CACHED = 2 * NY * CROWS
FRESH = 2 * NY * NROWS
CHUNK = 256


def load_keys(pieces, keys, values):
    at = 0
    for first, count in ((0, CROWS), (CROWS, NROWS)):
        for ref in pieces:
            size = NY * count
            both = ref[:, first : first + count, :].reshape(size, 2 * ATT_DIM)
            keys[at : at + size, :] = both[:, :ATT_DIM]
            values[at : at + size, :ATT_DIM] = both[:, ATT_DIM:]
            at += size
    values[:, ATT_DIM:] = jnp.ones((NY * 2 * HALF, ATT_DIM), BF16)


def positions(place):
    col = lax.broadcasted_iota(jnp.int32, (1, FRESH), 1)
    base = jnp.zeros((1, FRESH), jnp.int32)
    for k in range(2 * NY):
        side = place[3] if k < NY else 1 - place[3]
        start = k % NY * TOK + side * NROWS - k * NROWS
        base = jnp.where(col >= k * NROWS, start, base)
    return col + base


def attend_kernel(own, place, *refs):
    count = 1 if own else NX - 1
    queries, pieces = refs[:count], refs[count : count + 2]
    outs = refs[count + 2 : 2 * count + 2]
    keys, values, q_rows, sums = refs[2 * count + 2 :]
    mine = place[0]
    load_keys(pieces, keys, values)
    for b in range(count):
        for h in range(QH):
            q_rows[b, h * TOK : (h + 1) * TOK, :] = queries[b][:, h * ATT_DIM : (h + 1) * ATT_DIM]

    def attend_block(b, last):
        q = q_rows[b]
        carry = None
        if own:
            pos = positions(place)
            row = lax.broadcasted_iota(jnp.int32, (TOK, 1), 0) + place[1] * TOK
            row = jnp.concatenate([row] * QH, axis=0)
        for at in range(0, last, CHUNK):
            scores = lax.dot_general(
                q, keys[at : at + CHUNK, :], (((1,), (1,)), ((), ())), preferred_element_type=F32
            )
            if own and at >= CACHED:
                seen = pos[:, at - CACHED : at - CACHED + CHUNK] <= row
                scores = jnp.where(seen, scores, NEG)
            best = jnp.max(jnp.maximum(scores[:, :128], scores[:, 128:]), axis=1, keepdims=True)
            top = best if carry is None else jnp.maximum(carry[1], best)
            probs = jnp.exp2(scores * SCALE - top * SCALE).astype(BF16)
            summed = jnp.dot(probs, values[at : at + CHUNK, :], preferred_element_type=F32)
            if carry is not None:
                summed += carry[0] * jnp.exp2((carry[1] - top) * SCALE)
            carry = (summed, top)
        summed, top = carry
        total = summed[:, ATT_DIM:]
        sums[b, :, :ATT_DIM] = summed[:, :ATT_DIM] / total
        sums[b, :, ATT_DIM:] = top * SCALE + jnp.log2(total)

    if own:
        attend_block(0, CACHED + FRESH)
    else:

        @pl.loop(0, count)
        def _(b):
            owner = lax.rem(mine + b + 1, NX)

            @pl.when(owner > mine)
            def _():
                attend_block(b, CACHED + FRESH)

            @pl.when(owner < mine)
            def _():
                attend_block(b, CACHED)

    peaks = jnp.max(pieces[0][:, HALF:, :].astype(F32), axis=0)
    peaks = jnp.concatenate(
        [peaks[r // 2 : r // 2 + 1, r % 2 * 128 : r % 2 * 128 + 128] for r in range(8)], axis=0
    )
    diagonal = lax.broadcasted_iota(jnp.int32, (128, 128), 0) == lax.broadcasted_iota(
        jnp.int32, (128, 128), 1
    )
    for b in range(count):
        outs[b][:ROWS, :] = sums[b, :, :ATT_DIM].astype(BF16)
        lines = []
        for k in range(ROWS // 128):
            part = sums[b, k * 128 : k * 128 + 128, ATT_DIM:]
            lines.append(jnp.sum(jnp.where(diagonal, part, 0.0), axis=0, keepdims=True))
        lines.append(jnp.zeros((2, ATT_DIM), F32))
        packed = [p.astype(F32) for p in parts_of(jnp.concatenate(lines, axis=0))]
        packed.append(peaks)
        outs[b][ROWS:, :] = jnp.concatenate(packed, axis=0).astype(BF16)


def attend(place, queries, pieces, name):
    count = len(queries)
    partial = jax.ShapeDtypeStruct((ROWS + STAT, ATT_DIM), BF16)
    return call(
        functools.partial(attend_kernel, count == 1),
        [partial] * count,
        (place, *queries, *pieces),
        name,
        60_000_000_000 if count > 1 else 4 * ROWS * (CACHED + FRESH) * ATT_DIM,
        scratch=(
            pltpu.VMEM((CACHED + FRESH, ATT_DIM), BF16),
            pltpu.VMEM((CACHED + FRESH, 2 * ATT_DIM), BF16),
            pltpu.VMEM((count, ROWS, ATT_DIM), BF16),
            pltpu.VMEM((count, ROWS, 2 * ATT_DIM), F32),
        ),
    )


def merge_kernel(place, *refs):
    parts, nk, out, codes, scale = refs[:NX], *refs[NX:]
    peaks = functools.reduce(jnp.maximum, [ref[ROWS:, :].astype(F32)[24:32] for ref in parts])
    peaks = jnp.concatenate([peaks[r : r + 1, :] for r in range(8)], axis=1)
    key_scale = (peaks + 1e-6) / 127.0
    scale[...] = key_scale
    codes[...] = (nk[...].astype(F32) / key_scale).astype(BF16)
    diagonal = lax.broadcasted_iota(jnp.int32, (128, 128), 0) == lax.broadcasted_iota(
        jnp.int32, (128, 128), 1
    )
    stats = []
    for ref in parts:
        packed = ref[ROWS:, :].astype(F32)
        stats.append(packed[0:8] + packed[8:16] + packed[16:24])
    top = functools.reduce(jnp.maximum, stats)
    shares = [jnp.exp2(s - top) for s in stats]
    total = functools.reduce(jnp.add, shares)
    shares = [s / total for s in shares]
    pieces = []
    for k in range(ROWS // 128):
        summed = jnp.zeros((128, 128), F32)
        for share, ref in zip(shares, parts):
            line = jnp.where(diagonal, share[k : k + 1, :], 0.0)
            column = jnp.sum(line, axis=1, keepdims=True)
            summed += column * ref[k * 128 : k * 128 + 128, :].astype(F32)
        pieces.append(summed)
    result = jnp.concatenate(pieces, axis=0)
    for h in range(QH):
        out[:, h * ATT_DIM : (h + 1) * ATT_DIM] = result[h * TOK : (h + 1) * TOK, :].astype(BF16)


def shift(value, axis, by):
    size = lax.axis_size(axis)
    return lax.ppermute(value, axis, [(i, (i + by) % size) for i in range(size)])


def body(
    ssm_input,
    state_in,
    state_out,
    step_size,
    decay_rate,
    forget,
    skip_gain,
    queries,
    new_keys,
    new_values,
    cache_keys,
    cache_values,
    cache_key_scale,
    cache_value_scale,
):
    head = lax.axis_index("head")
    step_t = step_size.T
    column, core = head // 2, head % 2
    place = jnp.stack(
        [lax.axis_index("seq_0"), lax.axis_index("seq_1"), column, core]
    ).astype(jnp.int32)

    packed = pack(
        place,
        cache_keys,
        cache_values,
        new_keys,
        new_values,
        cache_key_scale.reshape(1, -1),
        cache_value_scale.reshape(1, -1),
    )
    swap = [(i, i ^ 1) for i in range(lax.axis_size("head"))]
    kv_a = lax.all_to_all(packed, "seq_1", 0, 0, tiled=True)
    q_left = shift(queries, "seq_0", 1)
    q_right = shift(queries, "seq_0", -1)
    q_far = shift(queries, "seq_0", 2)

    b_map = lax.dynamic_slice_in_dim(state_in, column * STATE, STATE, 1)
    c_map = lax.dynamic_slice_in_dim(state_out, column * STATE, STATE, 1)
    send, running, run_t = call(
        local_kernel,
        [
            jax.ShapeDtypeStruct((ND, SLOT, 128), BF16),
            jax.ShapeDtypeStruct((TOK, HEADS), F32),
            jax.ShapeDtypeStruct((HEADS, TOK), F32),
        ],
        (
            place,
            ssm_input,
            step_t,
            b_map,
            decay_rate.reshape(1, -1),
            forget.reshape(1, -1),
        ),
        "local",
        2 * TOK * COLS * STATE,
        after=(packed,),
    )
    kv_a = hold(kv_a, (run_t, q_left, q_right, q_far))
    kv_b = lax.ppermute(kv_a, "head", swap)
    pieces = (kv_a, kv_b)
    send = hold(send, (kv_a,))
    recv = lax.all_to_all(send, SEQ, 0, 0, tiled=True)
    p_right, p_far, p_left = attend(
        place, (q_right, q_far, q_left), pieces, "attend_others"
    )
    (p_own,) = attend(place, (queries,), pieces, "attend_own")
    base = call(
        within_kernel,
        jax.ShapeDtypeStruct((TOK, COLS), F32),
        (place, ssm_input, step_t, running, run_t, b_map, c_map, skip_gain.reshape(1, -1)),
        "within",
        4 * TOK * COLS * TOK,
        after=(p_right,),
    )
    back = call(
        scan_kernel,
        jax.ShapeDtypeStruct((ND, BACK, 128), BF16),
        (place, recv),
        "scan",
        1000000,
        after=(base,),
    )
    carried = lax.all_to_all(back, SEQ, 0, 0, tiled=True)

    r_left = shift(p_left, "seq_0", -1)
    r_right = shift(p_right, "seq_0", 1)
    r_far = shift(p_far, "seq_0", 2)
    attended, key_codes, key_scale = call(
        merge_kernel,
        [
            jax.ShapeDtypeStruct((TOK, QH * ATT_DIM), BF16),
            jax.ShapeDtypeStruct((TOK, KV_HEADS * ATT_DIM), BF16),
            jax.ShapeDtypeStruct((1, KV_HEADS * ATT_DIM), F32),
        ],
        (place, p_own, r_far, r_right, r_left, new_keys),
        "merge",
        1000000,
    )
    ssm_output = call(
        final_kernel,
        jax.ShapeDtypeStruct((TOK, COLS), BF16),
        (place, carried, base, c_map, running),
        "final",
        2 * TOK * COLS * STATE,
        scratch=(pltpu.VMEM((STATE, COLS), BF16),),
    )
    return (ssm_output, attended, key_codes, key_scale.reshape(-1))


def solution(mesh):
    split = Mesh(mesh.devices.reshape(NX, NY, mesh.shape["head"]), ("seq_0", "seq_1", "head"))
    return jax.shard_map(
        body,
        mesh=split,
        in_specs=(
            P(SEQ, "head"),
            P(SEQ, None),
            P(SEQ, None),
            P(SEQ, "head"),
            P("head"),
            P(SEQ),
            P("head"),
            P(SEQ, "head"),
            P(SEQ, None),
            P(SEQ, None),
            P(SEQ, None),
            P(SEQ, None),
            P(),
            P(),
        ),
        out_specs=(P(SEQ, "head"), P(SEQ, "head"), P(SEQ, None), P()),
        check_vma=False,
    )
```
